32 devices in a mesh: row: 16 (over z, y, x), rhs: 2 (over core).
Axes of the slice: x: 2, y: 2, z: 4, core: 2. Of those that a mesh axis runs over, the one named last changes fastest.
Arguments:
- right_sides: float32 [64, 8, 1024], P('rhs', None, 'row'), parts along dimension 0, may hold values from -6 to 6
- lower_blocks: float32 [28, 1024, 1024], P(None, 'row'), may hold values from -0.078125 to 0.078125
- inverse_blocks: float32 [8, 1024, 1024], P(None, 'row'), may hold values from -1 to 1.2, as said below
Outputs:
- solution: float32 [64, 8, 1024], P('rhs', None, 'row'), parts along dimension 0
The draws below stay inside these ranges and needn't reach their ends.
There are 2 independent parts, one for each index of `rhs`. The reference program is written for one: setup_inputs(seed, part) draws one part's arguments, and reference() takes and returns one part's arrays. A program takes and returns all parts, laid end to end along the dimension named above; an argument that names none is the same for every part. Nothing has to cross between parts.
Inputs may be any that keep to these rules, and one draw needn't show every extreme that they name: `inverse_blocks`: each block is lower triangular with diagonal entries between 0.5 and 1.2.
All inputs are finite; a program needn't handle non-finite values.
Results may differ from the reference program's by a relative error of at most 0.0001.
Values sent between devices are 32-bit elements; how exact they have to be, the bound alone decides.
A program may use at most 64 MiB of HBM per device.

```python
import math
import jax
import jax.numpy as jnp
from jax import lax

BLOCK = 1024
WINDOW = 8
RHS = 32
PAIRS = 28


def draw_inverse_blocks(key, part):
    key = jax.random.fold_in(key, 11)
    key_off, key_diag = jax.random.split(key)
    shape_all = (WINDOW, BLOCK, BLOCK)
    rows_index = lax.broadcasted_iota(jnp.int32, shape_all, 1)
    cols_index = lax.broadcasted_iota(jnp.int32, shape_all, 2)
    below = (cols_index < rows_index).astype(jnp.float32)
    on_diagonal = (cols_index == rows_index).astype(jnp.float32)
    off_values = jax.random.truncated_normal(key_off, -4.0, 4.0, shape_all, jnp.float32) * (0.5 / math.sqrt(BLOCK))
    diag_values = jax.random.uniform(key_diag, shape_all, jnp.float32, 0.5, 1.2)
    return below * off_values + on_diagonal * diag_values


def shard_levels(key, dims, pieces, least, largest):
    def one(dim, blocks):
        draws = jax.random.uniform(jax.random.fold_in(jax.random.fold_in(key, 6), dim), (blocks,), jnp.float32, least / len(pieces), largest / len(pieces))
        return jnp.repeat(jnp.exp(draws), dims[dim] // blocks).reshape((-1,) + (1,) * (len(dims) - dim - 1))

    factor_of = one(*pieces[0])
    for cut in pieces[1:]:
        factor_of = factor_of * one(*cut)
    return factor_of


def normal_values(own_key, dims, deviation, bound, cuts=(), dtype=jnp.bfloat16):
    array = deviation * jax.random.normal(own_key, dims, jnp.float32)
    if cuts:
        array = array * shard_levels(own_key, dims, cuts, -0.22, 0.18)
    return jnp.clip(array, -bound, bound).astype(dtype)


def setup_inputs(seed: int = 0, part: int = 0) -> dict:
    streams_of = jax.random.split(jax.random.key(seed), 4)
    part_splits = jax.random.split(jax.random.fold_in(streams_of[3], part), 4)
    right_sides = normal_values(part_splits[0], (RHS, WINDOW, BLOCK), 1.0, 6.0, ((2, 16),), jnp.float32)
    lower_blocks = normal_values(streams_of[1], (PAIRS, BLOCK, BLOCK), (6 * BLOCK) ** -0.5, 0.078125, ((1, 16),), jnp.float32)
    inverse_blocks = draw_inverse_blocks(jax.random.fold_in(streams_of[3], 71), part)
    return {"right_sides": right_sides, "lower_blocks": lower_blocks, "inverse_blocks": inverse_blocks}


def apply_rows(left, right):
    return lax.dot_general(left, right, (((1,), (1,)), ((), ())), precision=lax.Precision.HIGHEST, preferred_element_type=jnp.float32)


def reference(right_sides, lower_blocks, inverse_blocks):
    solved = []
    for current in range(WINDOW):
        residual = right_sides[:, current, :]
        for earlier in range(current):
            index_pair = current * (current - 1) // 2 + earlier
            residual = residual - apply_rows(solved[earlier], lower_blocks[index_pair])
        solved.append(apply_rows(residual, inverse_blocks[current]))
    return jnp.stack(solved, axis=1)
```

```python
import functools

import jax
import jax.numpy as jnp
from jax import lax
from jax.experimental import pallas as pl
from jax.experimental.pallas import tpu as pltpu
from jax.sharding import PartitionSpec as P

MESH = pl.DeviceIdType.MESH
LANES = 128
PIECE = 16


def split(value):
    high = value.astype(jnp.bfloat16)
    low = (value - high.astype(jnp.float32)).astype(jnp.bfloat16)
    return high, low


def dot(left, right):
    return jnp.dot(left, right, preferred_element_type=jnp.float32)


def kernel(
    n, window, rhs, rows, b_ref, l_ref, inv_ref, o_ref,
    l_raw, inv_raw, l_hi, l_lo, inv_hi, inv_lo, held, x_hi, x_lo, total,
    l_sem, inv_sem, send_sem, recv_sem,
):
    me = lax.axis_index("row")
    fold = rows // PIECE

    inv_copies = []
    l_copies = []
    for j in range(window):
        copy = pltpu.make_async_copy(inv_ref.at[j], inv_raw.at[j], inv_sem.at[j])
        copy.start()
        inv_copies.append(copy)
        if j + 1 < window:
            k = j + 1
            part = pl.ds(k * (k - 1) // 2, k)
            copy = pltpu.make_async_copy(l_ref.at[part], l_raw.at[part], l_sem.at[j])
            copy.start()
            l_copies.append(copy)

    barrier = pltpu.get_barrier_semaphore()
    for d in range(1, n):
        pl.semaphore_signal(
            barrier, inc=1, device_id={"row": lax.rem(me + d, n)}, device_id_type=MESH
        )

    for j in range(window):
        mine = b_ref[:, j, :]
        mine = jnp.concatenate(
            [mine, jnp.zeros((LANES - rhs, rows), jnp.float32)], axis=0
        )
        total[j] = mine.T

    pl.semaphore_wait(barrier, n - 1)

    lane = lax.broadcasted_iota(jnp.int32, (PIECE, LANES), 1)

    def send(phase, value):
        piece = value[0:PIECE]
        for g in range(1, fold):
            moved = pltpu.roll(value[g * PIECE:(g + 1) * PIECE], g * rhs, 1)
            piece = jnp.where(lane < g * rhs, piece, moved)
        held[phase, me] = piece
        for d in range(1, n):
            pltpu.make_async_remote_copy(
                src_ref=held.at[phase, me],
                dst_ref=held.at[phase, me],
                send_sem=send_sem.at[phase],
                recv_sem=recv_sem.at[phase],
                device_id={"row": lax.rem(me + d, n)},
                device_id_type=MESH,
            ).start()

    def all_of(phase):
        part = held.at[phase, pl.ds(0, n - 1)]
        return pltpu.make_async_remote_copy(
            src_ref=part,
            dst_ref=part,
            send_sem=send_sem.at[phase],
            recv_sem=recv_sem.at[phase],
            device_id={"row": lax.rem(me + 1, n)},
            device_id_type=MESH,
        )

    def receive(phase):
        all_of(phase).wait_recv()
        for q in range(n):
            piece = held[phase, q]
            for g in range(fold):
                part = piece if g == 0 else pltpu.roll(piece, LANES - g * rhs, 1)
                high, low = split(part)
                at = q * rows + g * PIECE
                x_hi[at:at + PIECE, :] = high
                x_lo[at:at + PIECE, :] = low

    def apply(high, low):
        return dot(high, x_hi[...]) + dot(low, x_hi[...]) + dot(high, x_lo[...])

    def pair(j, i):
        return j * (j - 1) // 2 + i

    for j in range(window):
        send(2 * j, total[j])
        inv_copies[j].wait()
        inv_hi[j], inv_lo[j] = split(inv_raw[j])
        if j + 1 < window:
            if j < 2:
                l_copies[j].wait()
            l_hi[j], l_lo[j] = split(l_raw[pair(j + 1, j)])
        if j > 0:
            for k in range(j + 1, window):
                if j == 1 and k > j + 1:
                    l_copies[k - 1].wait()
                high, low = split(l_raw[pair(k, j - 1)])
                total[k] = total[k] - apply(high, low)
        receive(2 * j)
        value = apply(inv_hi[j], inv_lo[j])
        if j + 1 < window:
            send(2 * j + 1, value)
        o_ref[:, j, :] = value.T[0:rhs]
        if j + 1 < window:
            receive(2 * j + 1)
            total[j + 1] = total[j + 1] - apply(l_hi[j], l_lo[j])

    for phase in range(2 * window - 1):
        all_of(phase).wait_send()


def body(right_sides, lower_blocks, inverse_blocks):
    n = lax.axis_size("row")
    rhs, window, rows = right_sides.shape
    pairs, _, size = lower_blocks.shape
    phases = 2 * window - 1
    return pl.pallas_call(
        functools.partial(kernel, n, window, rhs, rows),
        out_shape=jax.ShapeDtypeStruct(right_sides.shape, jnp.float32),
        in_specs=[
            pl.BlockSpec(memory_space=pltpu.VMEM),
            pl.BlockSpec(memory_space=pl.ANY),
            pl.BlockSpec(memory_space=pl.ANY),
        ],
        out_specs=pl.BlockSpec(memory_space=pltpu.VMEM),
        scratch_shapes=[
            pltpu.VMEM((pairs, rows, size), jnp.float32),
            pltpu.VMEM((window, rows, size), jnp.float32),
            pltpu.VMEM((window, rows, size), jnp.bfloat16),
            pltpu.VMEM((window, rows, size), jnp.bfloat16),
            pltpu.VMEM((window, rows, size), jnp.bfloat16),
            pltpu.VMEM((window, rows, size), jnp.bfloat16),
            pltpu.VMEM((phases, n, PIECE, LANES), jnp.float32),
            pltpu.VMEM((size, LANES), jnp.bfloat16),
            pltpu.VMEM((size, LANES), jnp.bfloat16),
            pltpu.VMEM((window, rows, LANES), jnp.float32),
            pltpu.SemaphoreType.DMA((window,)),
            pltpu.SemaphoreType.DMA((window,)),
            pltpu.SemaphoreType.DMA((phases,)),
            pltpu.SemaphoreType.DMA((phases,)),
        ],
        compiler_params=pltpu.CompilerParams(
            collective_id=0, has_side_effects=True, vmem_limit_bytes=40 << 20
        ),
    )(right_sides, lower_blocks, inverse_blocks)


def solution(mesh):
    return jax.shard_map(
        body,
        mesh=mesh,
        in_specs=(P("rhs", None, "row"), P(None, "row", None), P(None, "row", None)),
        out_specs=P("rhs", None, "row"),
        check_vma=False,
    )
```

```python
import functools

import jax
import jax.numpy as jnp
from jax import lax
from jax.experimental import pallas as pl
from jax.experimental.pallas import tpu as pltpu
from jax.sharding import PartitionSpec as P

MESH = pl.DeviceIdType.MESH
LANES = 128
PIECE = 16
CHUNK = 256


def split(value):
    high = value.astype(jnp.bfloat16)
    low = (value - high.astype(jnp.float32)).astype(jnp.bfloat16)
    return high, low


def dot(left, right):
    return jnp.dot(left, right, preferred_element_type=jnp.float32)


def kernel(
    n, window, rhs, rows, b_ref, l_ref, inv_ref, o_ref,
    l_raw, inv_raw, l_hi, l_lo, inv_hi, inv_lo, held, x_hi, x_lo, total,
    l_sem, inv_sem, send_sem, recv_sem,
):
    me = lax.axis_index("row")
    fold = rows // PIECE
    group = CHUNK // rows
    groups = n // group
    mine, place = me // group, lax.rem(me, group)

    inv_copies = []
    l_copies = []
    for j in range(window):
        copy = pltpu.make_async_copy(inv_ref.at[j], inv_raw.at[j], inv_sem.at[j])
        copy.start()
        inv_copies.append(copy)
        if j + 1 < window:
            k = j + 1
            part = pl.ds(k * (k - 1) // 2, k)
            copy = pltpu.make_async_copy(l_ref.at[part], l_raw.at[part], l_sem.at[j])
            copy.start()
            l_copies.append(copy)

    barrier = pltpu.get_barrier_semaphore()
    for d in range(1, n):
        pl.semaphore_signal(
            barrier, inc=1, device_id={"row": lax.rem(me + d, n)}, device_id_type=MESH
        )

    for j in range(window):
        part = b_ref[:, j, :]
        part = jnp.concatenate(
            [part, jnp.zeros((LANES - rhs, rows), jnp.float32)], axis=0
        )
        total[j] = part.T

    pl.semaphore_wait(barrier, n - 1)

    def partner(d):
        if groups != 4:
            return lax.rem(mine + d, groups)
        if d == 1:
            return mine + 1 - 2 * lax.rem(mine, 2)
        return (mine, None, lax.rem(mine + 2, 4), 3 - mine)[d]

    lane = lax.broadcasted_iota(jnp.int32, (PIECE, LANES), 1)

    def send(phase, value):
        piece = value[0:PIECE]
        for g in range(1, fold):
            moved = pltpu.roll(value[g * PIECE:(g + 1) * PIECE], g * rhs, 1)
            piece = jnp.where(lane < g * rhs, piece, moved)
        held[phase, me] = piece
        for d in reversed(range(groups)):
            other = partner(d)
            for e in reversed(range(group)):
                if d == 0 and e == 0:
                    continue
                target = other * group + lax.rem(place + e, group)
                pltpu.make_async_remote_copy(
                    src_ref=held.at[phase, me],
                    dst_ref=held.at[phase, me],
                    send_sem=send_sem.at[phase],
                    recv_sem=recv_sem.at[phase, mine],
                    device_id={"row": target},
                    device_id_type=MESH,
                ).start()

    def all_of(phase, source, count):
        part = held.at[phase, pl.ds(0, count)]
        return pltpu.make_async_remote_copy(
            src_ref=part,
            dst_ref=part,
            send_sem=send_sem.at[phase],
            recv_sem=recv_sem.at[phase, source],
            device_id={"row": lax.rem(me + 1, n)},
            device_id_type=MESH,
        )

    def receive(phase, high, low):
        side = phase % 2
        result = None
        for d in range(groups):
            source = partner(d)
            all_of(phase, source, group - 1 if d == 0 else group).wait_recv()
            highs, lows = [], []
            for k in range(group):
                piece = held[phase, source * group + k]
                for g in range(fold):
                    part = piece if g == 0 else pltpu.roll(piece, LANES - g * rhs, 1)
                    one, two = split(part)
                    highs.append(one)
                    lows.append(two)
            right_high = jnp.concatenate(highs, axis=0)
            right_low = jnp.concatenate(lows, axis=0)
            at = pl.ds(pl.multiple_of(source * CHUNK, CHUNK), CHUNK)
            if side:
                x_hi[at, :] = right_high
                x_lo[at, :] = right_low
            left_high, left_low = high[:, at], low[:, at]
            term = dot(left_high, right_high) + dot(left_low, right_high)
            term = term + dot(left_high, right_low)
            result = term if result is None else result + term
        return result

    def apply(high, low):
        return dot(high, x_hi[...]) + dot(low, x_hi[...]) + dot(high, x_lo[...])

    def older(j, first, last):
        for k in range(first, last):
            if j == 1:
                l_copies[k - 1].wait()
            high, low = split(l_raw[pair(k, j - 1)])
            total[k] = total[k] - apply(high, low)

    def pair(j, i):
        return j * (j - 1) // 2 + i

    for j in range(window):
        send(2 * j, total[j])
        inv_copies[j].wait()
        inv_hi[j], inv_lo[j] = split(inv_raw[j])
        middle = j + 1 + (window - j) // 2
        if j > 0:
            older(j, j + 1, min(middle, window))
        value = receive(2 * j, inv_hi.at[j], inv_lo.at[j])
        if j + 1 < window:
            send(2 * j + 1, value)
        o_ref[:, j, :] = value.T[0:rhs]
        if j + 1 < window:
            if j == 0:
                l_copies[j].wait()
            l_hi[j], l_lo[j] = split(l_raw[pair(j + 1, j)])
            if j > 0:
                older(j, middle, window)
            total[j + 1] = total[j + 1] - receive(2 * j + 1, l_hi.at[j], l_lo.at[j])

    for phase in range(2 * window - 1):
        all_of(phase, 0, n - 1).wait_send()


def body(right_sides, lower_blocks, inverse_blocks):
    n = lax.axis_size("row")
    rhs, window, rows = right_sides.shape
    pairs, _, size = lower_blocks.shape
    phases = 2 * window - 1
    return pl.pallas_call(
        functools.partial(kernel, n, window, rhs, rows),
        out_shape=jax.ShapeDtypeStruct(right_sides.shape, jnp.float32),
        in_specs=[
            pl.BlockSpec(memory_space=pltpu.VMEM),
            pl.BlockSpec(memory_space=pl.ANY),
            pl.BlockSpec(memory_space=pl.ANY),
        ],
        out_specs=pl.BlockSpec(memory_space=pltpu.VMEM),
        scratch_shapes=[
            pltpu.VMEM((pairs, rows, size), jnp.float32),
            pltpu.VMEM((window, rows, size), jnp.float32),
            pltpu.VMEM((window, rows, size), jnp.bfloat16),
            pltpu.VMEM((window, rows, size), jnp.bfloat16),
            pltpu.VMEM((window, rows, size), jnp.bfloat16),
            pltpu.VMEM((window, rows, size), jnp.bfloat16),
            pltpu.VMEM((phases, n, PIECE, LANES), jnp.float32),
            pltpu.VMEM((size, LANES), jnp.bfloat16),
            pltpu.VMEM((size, LANES), jnp.bfloat16),
            pltpu.VMEM((window, rows, LANES), jnp.float32),
            pltpu.SemaphoreType.DMA((window,)),
            pltpu.SemaphoreType.DMA((window,)),
            pltpu.SemaphoreType.DMA((phases,)),
            pltpu.SemaphoreType.DMA((phases, n * rows // CHUNK)),
        ],
        compiler_params=pltpu.CompilerParams(
            collective_id=0, has_side_effects=True, vmem_limit_bytes=40 << 20
        ),
    )(right_sides, lower_blocks, inverse_blocks)


def solution(mesh):
    return jax.shard_map(
        body,
        mesh=mesh,
        in_specs=(P("rhs", None, "row"), P(None, "row", None), P(None, "row", None)),
        out_specs=P("rhs", None, "row"),
        check_vma=False,
    )
```

```python
import functools

import jax
import jax.numpy as jnp
from jax import lax
from jax.experimental import pallas as pl
from jax.experimental.pallas import tpu as pltpu
from jax.sharding import PartitionSpec as P

MESH = pl.DeviceIdType.MESH
LANES = 128
PIECE = 16
CHUNK = 256


def split(value):
    high = value.astype(jnp.bfloat16)
    low = (value - high.astype(jnp.float32)).astype(jnp.bfloat16)
    return high, low


def dot(left, right):
    return jnp.dot(left, right, preferred_element_type=jnp.float32)


def kernel(
    n, window, rhs, rows, b_ref, l_ref, inv_ref, o_ref,
    l_raw, inv_raw, l_hi, l_lo, inv_hi, inv_lo, held, x_hi, x_lo, total,
    l_sem, inv_sem, send_sem, recv_sem,
):
    me = lax.axis_index("row")
    fold = rows // PIECE
    group = CHUNK // rows
    groups = n // group
    mine, place = me // group, lax.rem(me, group)

    inv_copies = []
    l_copies = []
    for j in range(window):
        copy = pltpu.make_async_copy(inv_ref.at[j], inv_raw.at[j], inv_sem.at[j])
        copy.start()
        inv_copies.append(copy)
        if j + 1 < window:
            k = j + 1
            part = pl.ds(k * (k - 1) // 2, k)
            copy = pltpu.make_async_copy(l_ref.at[part], l_raw.at[part], l_sem.at[j])
            copy.start()
            l_copies.append(copy)

    barrier = pltpu.get_barrier_semaphore()
    for d in range(1, n):
        pl.semaphore_signal(
            barrier, inc=1, device_id={"row": lax.rem(me + d, n)}, device_id_type=MESH
        )

    for j in range(window):
        part = b_ref[:, j, :]
        part = jnp.concatenate(
            [part, jnp.zeros((LANES - rhs, rows), jnp.float32)], axis=0
        )
        total[j] = part.T

    for later in range(1, groups):
        @pl.when(later > mine)
        def _(later=later):
            for j in range(window):
                held[2 * j, later * group:(later + 1) * group] = jnp.zeros(
                    (group, PIECE, LANES), jnp.float32
                )

    pl.semaphore_wait(barrier, n - 1)

    def partner(d):
        if groups != 4:
            return lax.rem(mine + d, groups)
        if d == 1:
            return mine + 1 - 2 * lax.rem(mine, 2)
        return (mine, None, lax.rem(mine + 2, 4), 3 - mine)[d]

    lane = lax.broadcasted_iota(jnp.int32, (PIECE, LANES), 1)

    def send(phase, value):
        piece = value[0:PIECE]
        for g in range(1, fold):
            moved = pltpu.roll(value[g * PIECE:(g + 1) * PIECE], g * rhs, 1)
            piece = jnp.where(lane < g * rhs, piece, moved)
        held[phase, me] = piece
        for d in reversed(range(groups)):
            other = partner(d)

            def to_group(d=d, other=other):
                for e in reversed(range(group)):
                    if d == 0 and e == 0:
                        continue
                    pltpu.make_async_remote_copy(
                        src_ref=held.at[phase, me],
                        dst_ref=held.at[phase, me],
                        send_sem=send_sem.at[phase, d],
                        recv_sem=recv_sem.at[phase, mine],
                        device_id={"row": other * group + lax.rem(place + e, group)},
                        device_id_type=MESH,
                    ).start()

            if d == 0 or phase % 2:
                to_group()
            else:
                pl.when(other > mine)(to_group)

    def all_of(phase, source, d):
        part = held.at[phase, pl.ds(0, group - 1 if d == 0 else group)]
        return pltpu.make_async_remote_copy(
            src_ref=part,
            dst_ref=part,
            send_sem=send_sem.at[phase, d],
            recv_sem=recv_sem.at[phase, source],
            device_id={"row": lax.rem(me + 1, n)},
            device_id_type=MESH,
        )

    def receive(phase, high, low):
        side = phase % 2
        for d in range(groups):
            source = partner(d)
            copies = all_of(phase, source, d)
            if d == 0 or side:
                copies.wait_recv()
            else:
                pl.when(source < mine)(copies.wait_recv)
        result = None
        for d in range(groups):
            source = partner(d)
            highs, lows = [], []
            for k in range(group):
                piece = held[phase, source * group + k]
                for g in range(fold):
                    part = piece if g == 0 else pltpu.roll(piece, LANES - g * rhs, 1)
                    one, two = split(part)
                    highs.append(one)
                    lows.append(two)
            right_high = jnp.concatenate(highs, axis=0)
            right_low = jnp.concatenate(lows, axis=0)
            at = pl.ds(pl.multiple_of(source * CHUNK, CHUNK), CHUNK)
            if side:
                x_hi[at, :] = right_high
                x_lo[at, :] = right_low
            left_high, left_low = high[:, at], low[:, at]
            term = dot(left_high, right_high) + dot(left_low, right_high)
            term = term + dot(left_high, right_low)
            result = term if result is None else result + term
        return result

    def apply(high, low):
        return dot(high, x_hi[...]) + dot(low, x_hi[...]) + dot(high, x_lo[...])

    def older(j, first, last):
        for k in range(first, last):
            if j == 1:
                l_copies[k - 1].wait()
            high, low = split(l_raw[pair(k, j - 1)])
            total[k] = total[k] - apply(high, low)

    def pair(j, i):
        return j * (j - 1) // 2 + i

    for j in range(window):
        send(2 * j, total[j])
        inv_copies[j].wait()
        inv_hi[j], inv_lo[j] = split(inv_raw[j])
        middle = j + 1 + (window - j) // 2
        if j > 0:
            older(j, j + 1, min(middle, window))
        value = receive(2 * j, inv_hi.at[j], inv_lo.at[j])
        if j + 1 < window:
            send(2 * j + 1, value)
        o_ref[:, j, :] = value.T[0:rhs]
        if j + 1 < window:
            if j == 0:
                l_copies[j].wait()
            l_hi[j], l_lo[j] = split(l_raw[pair(j + 1, j)])
            if j > 0:
                older(j, middle, window)
            total[j + 1] = total[j + 1] - receive(2 * j + 1, l_hi.at[j], l_lo.at[j])

    for phase in range(2 * window - 1):
        for d in range(groups):
            other = partner(d)
            copies = all_of(phase, other, d)
            if d == 0 or phase % 2:
                copies.wait_send()
            else:
                pl.when(other > mine)(copies.wait_send)


def body(right_sides, lower_blocks, inverse_blocks):
    n = lax.axis_size("row")
    rhs, window, rows = right_sides.shape
    pairs, _, size = lower_blocks.shape
    phases = 2 * window - 1
    return pl.pallas_call(
        functools.partial(kernel, n, window, rhs, rows),
        out_shape=jax.ShapeDtypeStruct(right_sides.shape, jnp.float32),
        in_specs=[
            pl.BlockSpec(memory_space=pltpu.VMEM),
            pl.BlockSpec(memory_space=pl.ANY),
            pl.BlockSpec(memory_space=pl.ANY),
        ],
        out_specs=pl.BlockSpec(memory_space=pltpu.VMEM),
        scratch_shapes=[
            pltpu.VMEM((pairs, rows, size), jnp.float32),
            pltpu.VMEM((window, rows, size), jnp.float32),
            pltpu.VMEM((window, rows, size), jnp.bfloat16),
            pltpu.VMEM((window, rows, size), jnp.bfloat16),
            pltpu.VMEM((window, rows, size), jnp.bfloat16),
            pltpu.VMEM((window, rows, size), jnp.bfloat16),
            pltpu.VMEM((phases, n, PIECE, LANES), jnp.float32),
            pltpu.VMEM((size, LANES), jnp.bfloat16),
            pltpu.VMEM((size, LANES), jnp.bfloat16),
            pltpu.VMEM((window, rows, LANES), jnp.float32),
            pltpu.SemaphoreType.DMA((window,)),
            pltpu.SemaphoreType.DMA((window,)),
            pltpu.SemaphoreType.DMA((phases, n * rows // CHUNK)),
            pltpu.SemaphoreType.DMA((phases, n * rows // CHUNK)),
        ],
        compiler_params=pltpu.CompilerParams(
            collective_id=0, has_side_effects=True, vmem_limit_bytes=40 << 20
        ),
    )(right_sides, lower_blocks, inverse_blocks)


def solution(mesh):
    return jax.shard_map(
        body,
        mesh=mesh,
        in_specs=(P("rhs", None, "row"), P(None, "row", None), P(None, "row", None)),
        out_specs=P("rhs", None, "row"),
        check_vma=False,
    )
```

```python
import functools

import jax
import jax.numpy as jnp
from jax import lax
from jax.experimental import pallas as pl
from jax.experimental.pallas import tpu as pltpu
from jax.sharding import PartitionSpec as P

MESH = pl.DeviceIdType.MESH
LANES = 128
PIECE = 16
CHUNK = 256


def split(value):
    high = value.astype(jnp.bfloat16)
    low = (value - high.astype(jnp.float32)).astype(jnp.bfloat16)
    return high, low


def dot(left, right):
    return jnp.dot(left, right, preferred_element_type=jnp.float32)


def kernel(
    n, window, rhs, rows, b_ref, l_ref, inv_ref, o_ref,
    l_raw, inv_raw, l_hi, l_lo, inv_hi, inv_lo, held, x_hi, x_lo, total,
    l_sem, inv_sem, send_sem, recv_sem,
):
    me = lax.axis_index("row")
    fold = rows // PIECE
    group = CHUNK // rows
    groups = n // group
    mine, place = me // group, lax.rem(me, group)

    inv_copies = []
    l_copies = []
    for j in range(window):
        copy = pltpu.make_async_copy(inv_ref.at[j], inv_raw.at[j], inv_sem.at[j])
        copy.start()
        inv_copies.append(copy)
        if j + 1 < window:
            k = j + 1
            part = pl.ds(k * (k - 1) // 2, k)
            copy = pltpu.make_async_copy(l_ref.at[part], l_raw.at[part], l_sem.at[j])
            copy.start()
            l_copies.append(copy)

    barrier = pltpu.get_barrier_semaphore()
    for d in range(1, n):
        pl.semaphore_signal(
            barrier, inc=1, device_id={"row": lax.rem(me + d, n)}, device_id_type=MESH
        )

    for j in range(window):
        part = b_ref[:, j, :]
        part = jnp.concatenate(
            [part, jnp.zeros((LANES - rhs, rows), jnp.float32)], axis=0
        )
        total[j] = part.T

    for later in range(1, groups):
        @pl.when(later > mine)
        def _(later=later):
            for j in range(window):
                held[2 * j, later * group:(later + 1) * group] = jnp.zeros(
                    (group, PIECE, LANES), jnp.float32
                )

    pl.semaphore_wait(barrier, n - 1)

    def partner(d):
        if groups != 4:
            return lax.rem(mine + d, groups)
        if d == 1:
            return mine + 1 - 2 * lax.rem(mine, 2)
        return (mine, None, lax.rem(mine + 2, 4), 3 - mine)[d]

    lane = lax.broadcasted_iota(jnp.int32, (PIECE, LANES), 1)

    def send(phase, value):
        piece = value[0:PIECE]
        for g in range(1, fold):
            moved = pltpu.roll(value[g * PIECE:(g + 1) * PIECE], g * rhs, 1)
            piece = jnp.where(lane < g * rhs, piece, moved)
        held[phase, me] = piece
        for d in reversed(range(groups)):
            other = partner(d)

            def to_group(d=d, other=other):
                for e in reversed(range(group)):
                    if d == 0 and e == 0:
                        continue
                    pltpu.make_async_remote_copy(
                        src_ref=held.at[phase, me],
                        dst_ref=held.at[phase, me],
                        send_sem=send_sem.at[phase, d],
                        recv_sem=recv_sem.at[phase, mine],
                        device_id={"row": other * group + lax.rem(place + e, group)},
                        device_id_type=MESH,
                    ).start()

            if d == 0 or phase % 2:
                to_group()
            else:
                pl.when(other > mine)(to_group)

    def all_of(phase, source, d):
        part = held.at[phase, pl.ds(0, group - 1 if d == 0 else group)]
        return pltpu.make_async_remote_copy(
            src_ref=part,
            dst_ref=part,
            send_sem=send_sem.at[phase, d],
            recv_sem=recv_sem.at[phase, source],
            device_id={"row": lax.rem(me + 1, n)},
            device_id_type=MESH,
        )

    def receive(phase, high, low):
        side = phase % 2
        def arrive(d):
            source = partner(d)
            copies = all_of(phase, source, d)
            if d == 0 or side:
                copies.wait_recv()
            else:
                pl.when(source < mine)(copies.wait_recv)

        arrive(0)
        arrive(1)
        result = None
        for d in range(groups):
            if d == 2:
                arrive(2)
                arrive(3)
            source = partner(d)
            highs, lows = [], []
            for k in range(group):
                piece = held[phase, source * group + k]
                for g in range(fold):
                    part = piece if g == 0 else pltpu.roll(piece, LANES - g * rhs, 1)
                    one, two = split(part)
                    highs.append(one)
                    lows.append(two)
            right_high = jnp.concatenate(highs, axis=0)
            right_low = jnp.concatenate(lows, axis=0)
            at = pl.ds(pl.multiple_of(source * CHUNK, CHUNK), CHUNK)
            if side:
                x_hi[at, :] = right_high
                x_lo[at, :] = right_low
            left_high, left_low = high[:, at], low[:, at]
            both = dot(jnp.concatenate([left_high, left_low], axis=0), right_high)
            term = both[:rows] + both[rows:] + dot(left_high, right_low)
            result = term if result is None else result + term
        return result

    def apply(high, low):
        return dot(high, x_hi[...]) + dot(low, x_hi[...]) + dot(high, x_lo[...])

    def older(j, first, last):
        for k in range(first, last):
            if j == 1:
                l_copies[k - 1].wait()
            high, low = split(l_raw[pair(k, j - 1)])
            total[k] = total[k] - apply(high, low)

    def pair(j, i):
        return j * (j - 1) // 2 + i

    for j in range(window):
        send(2 * j, total[j])
        inv_copies[j].wait()
        inv_hi[j], inv_lo[j] = split(inv_raw[j])
        middle = j + 1 + (window - j) // 2
        if j > 0:
            older(j, j + 1, min(middle, window))
        value = receive(2 * j, inv_hi.at[j], inv_lo.at[j])
        if j + 1 < window:
            send(2 * j + 1, value)
        o_ref[:, j, :] = value.T[0:rhs]
        if j + 1 < window:
            if j == 0:
                l_copies[j].wait()
            l_hi[j], l_lo[j] = split(l_raw[pair(j + 1, j)])
            if j > 0:
                older(j, middle, window)
            total[j + 1] = total[j + 1] - receive(2 * j + 1, l_hi.at[j], l_lo.at[j])

    for phase in range(2 * window - 1):
        for d in range(groups):
            other = partner(d)
            copies = all_of(phase, other, d)
            if d == 0 or phase % 2:
                copies.wait_send()
            else:
                pl.when(other > mine)(copies.wait_send)


def body(right_sides, lower_blocks, inverse_blocks):
    n = lax.axis_size("row")
    rhs, window, rows = right_sides.shape
    pairs, _, size = lower_blocks.shape
    phases = 2 * window - 1
    return pl.pallas_call(
        functools.partial(kernel, n, window, rhs, rows),
        out_shape=jax.ShapeDtypeStruct(right_sides.shape, jnp.float32),
        in_specs=[
            pl.BlockSpec(memory_space=pltpu.VMEM),
            pl.BlockSpec(memory_space=pl.ANY),
            pl.BlockSpec(memory_space=pl.ANY),
        ],
        out_specs=pl.BlockSpec(memory_space=pltpu.VMEM),
        scratch_shapes=[
            pltpu.VMEM((pairs, rows, size), jnp.float32),
            pltpu.VMEM((window, rows, size), jnp.float32),
            pltpu.VMEM((window, rows, size), jnp.bfloat16),
            pltpu.VMEM((window, rows, size), jnp.bfloat16),
            pltpu.VMEM((window, rows, size), jnp.bfloat16),
            pltpu.VMEM((window, rows, size), jnp.bfloat16),
            pltpu.VMEM((phases, n, PIECE, LANES), jnp.float32),
            pltpu.VMEM((size, LANES), jnp.bfloat16),
            pltpu.VMEM((size, LANES), jnp.bfloat16),
            pltpu.VMEM((window, rows, LANES), jnp.float32),
            pltpu.SemaphoreType.DMA((window,)),
            pltpu.SemaphoreType.DMA((window,)),
            pltpu.SemaphoreType.DMA((phases, n * rows // CHUNK)),
            pltpu.SemaphoreType.DMA((phases, n * rows // CHUNK)),
        ],
        compiler_params=pltpu.CompilerParams(
            collective_id=0, has_side_effects=True, vmem_limit_bytes=40 << 20
        ),
    )(right_sides, lower_blocks, inverse_blocks)


def solution(mesh):
    return jax.shard_map(
        body,
        mesh=mesh,
        in_specs=(P("rhs", None, "row"), P(None, "row", None), P(None, "row", None)),
        out_specs=P("rhs", None, "row"),
        check_vma=False,
    )
```
